32 devices in a mesh: sec: 2 (over core), ctx: 8 (over z, x), head: 2 (over y).
Axes of the slice: x: 2, y: 2, z: 4, core: 2. Of those that a mesh axis runs over, the one named last changes fastest.
Arguments:
- query_self: bfloat16 [1536, 2048], P('ctx', ('sec', 'head')), may hold values from -12 to 12
- key_self: bfloat16 [1536, 2048], P('ctx', ('sec', 'head')), may hold values from -6 to 6
- value_self: bfloat16 [1536, 2048], P('ctx', ('sec', 'head')), may hold values from -6 to 6
- query_cross: bfloat16 [1536, 2048], P('ctx', ('sec', 'head')), may hold values from -12 to 12
- neighbour_kv: bfloat16 [32, 128, 4096], P(('sec', 'ctx', 'head')), may hold values from -6 to 6
- neighbour_map: int32 [24, 2], P('ctx'), may hold values from 0 to 3, all different within a row
Outputs:
- self_out: bfloat16 [1536, 2048], P('ctx', ('sec', 'head'))
- cross_out: bfloat16 [1536, 2048], P('ctx', ('sec', 'head'))
The draws below stay inside these ranges and needn't reach their ends.
Inputs may be any that keep to these rules, and one draw needn't show every extreme that they name: `neighbour_map`: entry v of stretch c names slot v % 1 of the device at index v // 1 along sec+head that shares stretch c's context shard; a stretch's two entries differ.
All inputs are finite; a program needn't handle non-finite values.
Results may differ from the reference program's by a relative error of at most 0.0035.
Values may be sent and summed in bfloat16 or wider, within the bound.
A program may use at most 64 MiB of HBM per device.

```python
import math
import jax
import jax.numpy as jnp
from jax import lax

HD = 128
NH = 16
STRETCH = 64
NB_LEN = 128
NEIGH = 2
SLOTS = 1
SEQ = 1536
STRETCHES = 24
CPD = 3
GROUP = 4
HPD = 4
BLOCKS = 32
N_SEC = 2
N_CTX = 8
N_HEAD = 2


def draw_query_self(key, part):
    inner_key = jax.random.fold_in(key, 1)
    drawn = jnp.clip(3.0 * jax.random.normal(inner_key, (SEQ, NH * HD), jnp.float32), -12.0, 12.0)
    return drawn.astype(jnp.bfloat16)


def draw_key_self(key, part):
    inner_key = jax.random.fold_in(key, 2)
    drawn = jnp.clip(jax.random.normal(inner_key, (SEQ, NH * HD), jnp.float32), -6.0, 6.0)
    return drawn.astype(jnp.bfloat16)


def draw_query_cross(key, part):
    inner_key = jax.random.fold_in(key, 3)
    drawn = jnp.clip(3.0 * jax.random.normal(inner_key, (SEQ, NH * HD), jnp.float32), -12.0, 12.0)
    return drawn.astype(jnp.bfloat16)


def draw_neighbour_kv(key, part):
    inner_key = jax.random.fold_in(key, 4)
    drawn = jnp.clip(jax.random.normal(inner_key, (BLOCKS, NB_LEN, NH * 2 * HD), jnp.float32), -6.0, 6.0)
    return drawn.astype(jnp.bfloat16)


def level_of(key, dims, cuts, low, high):
    loudness = 1.0
    for axis_at, parts in cuts:
        steps = jax.random.uniform(jax.random.fold_in(jax.random.fold_in(key, 6), axis_at), (parts,), jnp.float32, low / len(cuts), high / len(cuts))
        loudness = loudness * jnp.repeat(jnp.exp(steps), dims[axis_at] // parts).reshape((-1,) + (1,) * (len(dims) - 1 - axis_at))
    return loudness


def different_ones(own_key, rows, count, top, lift):
    sequence = jax.random.permutation(jax.random.fold_in(own_key, 1), count)
    pull = sequence
    for power in range(3):
        pull = pull * pull // count
    pull = pull * lift // count
    tickets = jax.random.randint(jax.random.fold_in(own_key, 2), (rows, count), 0, 4096) + pull
    holders = jax.random.permutation(jax.random.fold_in(own_key, 3), rows)[jnp.arange(count) % rows]
    tickets = jnp.where(jnp.arange(rows)[:, None] == holders[None, :], 1 << 14, tickets)
    score = tickets * count + jnp.arange(count)
    return lax.top_k(score.astype(jnp.int32), top)[1].astype(jnp.int32)


def noise(key, shape, scale, limit, shards=(), kind=jnp.bfloat16):
    values = jax.random.normal(key, shape, jnp.float32) * scale
    if len(shards) > 0:
        values = level_of(key, shape, shards, -0.22, 0.18) * values
    return jnp.clip(values, min=-limit, max=limit).astype(kind)


def setup_inputs(seed: int = 0) -> dict:
    arg_keys = jax.random.split(jax.random.key(seed), 7)
    return {
        "query_self": draw_query_self(jax.random.fold_in(arg_keys[6], 71), 0),
        "key_self": draw_key_self(jax.random.fold_in(arg_keys[6], 71), 0),
        "value_self": noise(arg_keys[2], (SEQ, NH * HD), 1.0, 6.0, ((0, 8), (1, 4))),
        "query_cross": draw_query_cross(jax.random.fold_in(arg_keys[6], 71), 0),
        "neighbour_kv": draw_neighbour_kv(jax.random.fold_in(arg_keys[6], 71), 0),
        "neighbour_map": different_ones(arg_keys[5], STRETCHES, N_SEC * N_HEAD * SLOTS, NEIGH, 8192),
    }


MASKED_SCORE = -1e+30

def softmax_attend(scores, key_mask, value_rows):
    masked = jnp.where(key_mask, scores, MASKED_SCORE)
    row_top = lax.optimization_barrier(jnp.max(masked, axis=-1, keepdims=True))
    exp_scores = jnp.where(key_mask, jnp.exp(masked - row_top), 0.0)
    row_total = lax.optimization_barrier(jnp.sum(exp_scores, axis=-1))
    rounded = lax.optimization_barrier(exp_scores.astype(jnp.bfloat16))
    summed = jnp.einsum('hqk,khd->qhd', rounded.astype(jnp.float32), value_rows)
    return summed / jnp.transpose(row_total)[:, :, None]

def reference(query_self, key_self, value_self, query_cross, neighbour_kv, neighbour_map):
    score_scale = 1.0 / math.sqrt(HD)
    query_full = query_self.astype(jnp.float32).reshape(SEQ, NH, HD)
    key_full = key_self.astype(jnp.float32).reshape(SEQ, NH, HD)
    value_full = value_self.astype(jnp.float32).reshape(SEQ, NH, HD)
    block_rows = min(SEQ, 512)
    pieces = []
    for first_row in range(0, SEQ, block_rows):
        last_row = first_row + block_rows
        scores = jnp.einsum('qhd,khd->hqk', query_full[first_row:last_row], key_full[:last_row]) * score_scale
        query_pos = first_row + jnp.arange(block_rows, dtype=jnp.int32)
        key_pos = jnp.arange(last_row, dtype=jnp.int32)
        key_mask = key_pos[None, None, :] <= query_pos[None, :, None]
        pieces.append(softmax_attend(scores, key_mask, value_full[:last_row]))
    self_out = jnp.concatenate(pieces, axis=0).reshape(SEQ, NH * HD).astype(jnp.bfloat16)
    blocks_view = neighbour_kv.reshape(BLOCKS, NB_LEN, GROUP, 2, HPD, HD)
    neighbour_keys = blocks_view[:, :, :, 0].reshape(BLOCKS, NB_LEN, NH, HD)
    neighbour_values = blocks_view[:, :, :, 1].reshape(BLOCKS, NB_LEN, NH, HD)
    stretch_ids = jnp.arange(STRETCHES, dtype=jnp.int32)
    shard_ids = stretch_ids // CPD
    holder = neighbour_map // SLOTS
    position = neighbour_map % SLOTS
    section = holder // N_HEAD
    within = holder % N_HEAD
    block_ids = (((section * N_CTX + shard_ids[:, None]) * N_HEAD + within) * SLOTS + position).astype(jnp.int32)
    stretch_queries = query_cross.reshape(STRETCHES, STRETCH, NH, HD)

    def one_stretch(scanned):
        stretch_query, block_pair, stretch_id = scanned
        key_rows = jnp.take(neighbour_keys, block_pair, axis=0).reshape(NEIGH * NB_LEN, NH, HD).astype(jnp.float32)
        value_rows = jnp.take(neighbour_values, block_pair, axis=0).reshape(NEIGH * NB_LEN, NH, HD).astype(jnp.float32)
        scores = jnp.einsum('qhd,khd->hqk', stretch_query.astype(jnp.float32), key_rows) * score_scale
        key_mask = jnp.ones((1, 1, NEIGH * NB_LEN), dtype=jnp.bool_)
        attended = softmax_attend(scores, key_mask, value_rows)
        return jnp.where(stretch_id > 0, attended, 0.0)
    crossed = lax.map(one_stretch, (stretch_queries, block_ids, stretch_ids))
    cross_out = crossed.reshape(SEQ, NH * HD).astype(jnp.bfloat16)
    return (self_out, cross_out)
```

```python
import functools
import math

import jax
import jax.numpy as jnp
from jax import lax
from jax.experimental import pallas as pl
from jax.experimental.pallas import tpu as pltpu
from jax.sharding import PartitionSpec as P

HD = 128
STRETCH = 64
MASKED_SCORE = -1e30
MESH = pl.DeviceIdType.MESH
BASE2 = math.log2(math.e) / math.sqrt(HD)


def scores_of(queries, keys):
    return lax.dot_general(
        queries, keys, (((1,), (1,)), ((), ())), preferred_element_type=jnp.float32
    )


def attend(queries, keys, values, mask=None):
    scores = scores_of(queries, keys)
    if mask is not None:
        scores = jnp.where(mask, scores, MASKED_SCORE)
    top = jnp.max(scores, axis=-1, keepdims=True) * BASE2
    probs = jnp.exp2(scores * BASE2 - top)
    total = jnp.sum(probs, axis=-1, keepdims=True)
    summed = jnp.dot(probs.astype(jnp.bfloat16), values, preferred_element_type=jnp.float32)
    return summed, top, total


def kernel(
    sizes,
    map_ref,
    qs_ref,
    k_ref,
    v_ref,
    qc_ref,
    nb_ref,
    so_ref,
    co_ref,
    k_all,
    v_all,
    q_in,
    o_part,
    l_part,
    o_in,
    l_in,
    own_sum,
    own_top,
    own_total,
    nb_all,
    kv_send,
    kv_recv,
    q_send,
    q_recv,
    o_send,
    o_recv,
    nb_send,
    nb_recv,
    nb_own,
):
    n_sec, n_ctx, n_head = sizes
    half = n_ctx // 2
    rows, width = qs_ref.shape
    heads = width // HD
    group = n_sec * n_head
    slots = nb_ref.shape[0]

    sec, ctx, head = (lax.axis_index(a) for a in ("sec", "ctx", "head"))
    upper = ctx >= half
    mine = lax.rem(ctx, half)
    base = ctx - mine
    partner = lax.rem(ctx + half, n_ctx)
    within = sec * n_head + head

    def member(d):
        other = lax.rem(within + d, group)
        return other, {"sec": other // n_head, "head": lax.rem(other, n_head)}

    def peer(d):
        return base + lax.rem(mine + d, half)

    def cols(h):
        return slice(h * HD, (h + 1) * HD)

    barrier = pltpu.get_barrier_semaphore()
    for d in range(1, half):
        pl.semaphore_signal(barrier, inc=1, device_id={"ctx": peer(d)}, device_id_type=MESH)
    pl.semaphore_signal(barrier, inc=1, device_id={"ctx": partner}, device_id_type=MESH)
    for d in range(1, group):
        pl.semaphore_signal(barrier, inc=1, device_id=member(d)[1], device_id_type=MESH)
    pl.semaphore_wait(barrier, half - 1 + 1 + group - 1)

    def q_copy(h):
        return pltpu.make_async_remote_copy(
            src_ref=qs_ref.at[:, cols(h)],
            dst_ref=q_in.at[:, cols(h)],
            send_sem=q_send.at[h],
            recv_sem=q_recv.at[h],
            device_id={"ctx": partner},
            device_id_type=MESH,
        )

    def kv_copy(d, h, t):
        source, gathered = ((k_ref, k_all), (v_ref, v_all))[t]
        return pltpu.make_async_remote_copy(
            src_ref=source.at[:, cols(h)],
            dst_ref=gathered.at[mine, :, cols(h)],
            send_sem=kv_send.at[d - 1, h, t],
            recv_sem=kv_recv.at[d - 1, h, t],
            device_id={"ctx": peer(d)},
            device_id_type=MESH,
        )

    def o_copy(h, t):
        source, target = ((o_part.at[:, cols(h)], o_in.at[:, cols(h)]), (l_part.at[h], l_in.at[h]))[t]
        return pltpu.make_async_remote_copy(
            src_ref=source,
            dst_ref=target,
            send_sem=o_send.at[h, t],
            recv_sem=o_recv.at[h, t],
            device_id={"ctx": partner},
            device_id_type=MESH,
        )

    def nb_copy(d):
        other, place = member(d)
        start = pl.multiple_of(other * (2 * width), 2 * width)
        return pltpu.make_async_remote_copy(
            src_ref=nb_ref.at[:, :, pl.ds(start, 2 * width)],
            dst_ref=nb_all.at[pl.ds(within * slots, slots)],
            send_sem=nb_send.at[d - 1],
            recv_sem=nb_recv.at[d - 1],
            device_id=place,
            device_id_type=MESH,
        )

    for h in range(heads):
        pl.when(upper)(lambda h=h: q_copy(h).start())
        for d in range(1, half):
            for t in range(2):
                kv_copy(d, h, t).start()
        if h == 0:
            for d in range(1, group):
                nb_copy(d).start()
    own_nb = pltpu.make_async_copy(
        nb_ref.at[:, :, pl.ds(pl.multiple_of(within * (2 * width), 2 * width), 2 * width)],
        nb_all.at[pl.ds(within * slots, slots)],
        nb_own,
    )
    own_nb.start()
    k_all[mine] = k_ref[...]
    v_all[mine] = v_ref[...]

    def gathered_head(h):
        keys = k_all[:, :, cols(h)].reshape(half * rows, HD)
        values = v_all[:, :, cols(h)].reshape(half * rows, HD)
        return keys, values

    def wait_kv(h):
        for d in range(1, half):
            for t in range(2):
                kv_copy(d, h, t).wait_recv()

    def attend_own(h):
        keys, values = gathered_head(h)
        place = lax.broadcasted_iota(jnp.int32, (rows, half * rows), 1)
        position = lax.broadcasted_iota(jnp.int32, (rows, half * rows), 0) + mine * rows
        return attend(qs_ref[:, cols(h)], keys, values, place <= position)

    def cross():
        own_nb.wait()
        for d in range(1, group):
            nb_copy(d).wait_recv()
        for c in range(rows // STRETCH):
            picks = [map_ref[c, r] for r in range(map_ref.shape[1])]
            part = slice(c * STRETCH, (c + 1) * STRETCH)
            keep = jnp.logical_or(ctx > 0, c > 0)
            for h in range(heads):
                keys = jnp.concatenate([nb_all[v, :, cols(h)] for v in picks], axis=0)
                values = jnp.concatenate([nb_all[v, :, cols(heads + h)] for v in picks], axis=0)
                summed, _, total = attend(qc_ref[part, cols(h)], keys, values)
                co_ref[part, cols(h)] = jnp.where(keep, summed / total, 0.0).astype(co_ref.dtype)

    @pl.when(jnp.logical_not(upper))
    def _():
        for h in range(heads):
            wait_kv(h)
            q_copy(h).wait_recv()
            keys, values = gathered_head(h)
            summed, top, total = attend(q_in[:, cols(h)], keys, values)
            o_part[:, cols(h)] = (summed / total).astype(o_part.dtype)
            level = jnp.broadcast_to(top + jnp.log2(total), (rows, HD))
            l_part[h] = jnp.transpose(level)[:8]
            for t in range(2):
                o_copy(h, t).start()
            summed, _, total = attend_own(h)
            so_ref[:, cols(h)] = (summed / total).astype(so_ref.dtype)
        cross()
        for h in range(heads):
            for t in range(2):
                o_copy(h, t).wait_send()

    @pl.when(upper)
    def _():
        for h in range(heads):
            wait_kv(h)
            summed, top, total = attend_own(h)
            own_sum[h] = summed
            own_top[h] = jnp.broadcast_to(top, (rows, HD))
            own_total[h] = jnp.broadcast_to(total, (rows, HD))
        cross()
        for h in range(heads):
            for t in range(2):
                o_copy(h, t).wait_recv()
            level = jnp.transpose(jnp.broadcast_to(l_in[h, 0:1], (HD, rows)))
            top = own_top[h]
            peak = jnp.maximum(top, level)
            own, far = jnp.exp2(top - peak), jnp.exp2(level - peak)
            summed = own_sum[h] * own + o_in[:, cols(h)].astype(jnp.float32) * far
            so_ref[:, cols(h)] = (summed / (own_total[h] * own + far)).astype(so_ref.dtype)
        for h in range(heads):
            q_copy(h).wait_send()

    for h in range(heads):
        for d in range(1, half):
            for t in range(2):
                kv_copy(d, h, t).wait_send()
    for d in range(1, group):
        nb_copy(d).wait_send()


def on_device(sizes, query_self, key_self, value_self, query_cross, neighbour_kv, neighbour_map):
    rows, width = query_self.shape
    heads = width // HD
    half = sizes[1] // 2
    group = sizes[0] * sizes[2]
    slots, block_len, _ = neighbour_kv.shape
    bf16, f32 = jnp.bfloat16, jnp.float32
    vmem = pl.BlockSpec(memory_space=pltpu.VMEM)
    out = jax.ShapeDtypeStruct((rows, width), bf16)
    pairs = rows * rows * heads * (2 * half)
    return pl.pallas_call(
        functools.partial(kernel, sizes),
        out_shape=(out, out),
        in_specs=[pl.BlockSpec(memory_space=pltpu.SMEM)]
        + [vmem] * 4
        + [pl.BlockSpec(memory_space=pl.ANY)],
        out_specs=(vmem, vmem),
        scratch_shapes=[
            pltpu.VMEM((half, rows, width), bf16),
            pltpu.VMEM((half, rows, width), bf16),
            pltpu.VMEM((rows, width), bf16),
            pltpu.VMEM((rows, width), bf16),
            pltpu.VMEM((heads, 8, rows), f32),
            pltpu.VMEM((rows, width), bf16),
            pltpu.VMEM((heads, 8, rows), f32),
            pltpu.VMEM((heads, rows, HD), f32),
            pltpu.VMEM((heads, rows, HD), f32),
            pltpu.VMEM((heads, rows, HD), f32),
            pltpu.VMEM((group * slots, block_len, 2 * width), bf16),
            pltpu.SemaphoreType.DMA((half - 1, heads, 2)),
            pltpu.SemaphoreType.DMA((half - 1, heads, 2)),
            pltpu.SemaphoreType.DMA((heads,)),
            pltpu.SemaphoreType.DMA((heads,)),
            pltpu.SemaphoreType.DMA((heads, 2)),
            pltpu.SemaphoreType.DMA((heads, 2)),
            pltpu.SemaphoreType.DMA((group - 1,)),
            pltpu.SemaphoreType.DMA((group - 1,)),
            pltpu.SemaphoreType.DMA,
        ],
        compiler_params=pltpu.CompilerParams(
            collective_id=0, has_side_effects=True, vmem_limit_bytes=56 * 1024 * 1024
        ),
        cost_estimate=pl.CostEstimate(
            flops=4 * pairs * HD, bytes_accessed=2 * 1024 * 1024, transcendentals=pairs
        ),
    )(neighbour_map, query_self, key_self, value_self, query_cross, neighbour_kv)


def solution(mesh):
    sizes = tuple(mesh.shape[a] for a in ("sec", "ctx", "head"))
    split = P("ctx", ("sec", "head"))
    return jax.shard_map(
        functools.partial(on_device, sizes),
        mesh=mesh,
        in_specs=(split, split, split, split, P(("sec", "ctx", "head"), None, None), P("ctx", None)),
        out_specs=(split, split),
        check_vma=False,
    )
```

```python
import functools
import math

import jax
import jax.numpy as jnp
from jax import lax
from jax.experimental import pallas as pl
from jax.experimental.pallas import tpu as pltpu
from jax.sharding import PartitionSpec as P

HD = 128
STRETCH = 64
MASKED_SCORE = -1e30
AHEAD = 2
MESH = pl.DeviceIdType.MESH
BASE2 = math.log2(math.e) / math.sqrt(HD)


def scores_of(queries, keys):
    return lax.dot_general(
        queries, keys, (((1,), (1,)), ((), ())), preferred_element_type=jnp.float32
    )


def attend(queries, keys, values, mask=None):
    scores = scores_of(queries, keys)
    if mask is not None:
        scores = jnp.where(mask, scores, MASKED_SCORE)
    top = jnp.max(scores, axis=-1, keepdims=True) * BASE2
    probs = jnp.exp2(scores * BASE2 - top)
    total = jnp.sum(probs, axis=-1, keepdims=True)
    summed = jnp.dot(probs.astype(jnp.bfloat16), values, preferred_element_type=jnp.float32)
    return summed, top, total


def kernel(
    sizes,
    map_ref,
    qs_hbm,
    k_ref,
    v_ref,
    qc_hbm,
    nb_ref,
    so_hbm,
    co_hbm,
    qs_ref,
    qc_ref,
    so_ref,
    co_ref,
    k_all,
    v_all,
    q_in,
    o_part,
    l_part,
    o_in,
    l_in,
    own_sum,
    own_top,
    own_total,
    nb_all,
    kv_send,
    kv_recv,
    q_send,
    q_recv,
    o_send,
    o_recv,
    nb_send,
    nb_recv,
    load,
    store,
):
    n_sec, n_ctx, n_head = sizes
    half = n_ctx // 2
    rows, width = qs_ref.shape
    heads = width // HD
    group = n_sec * n_head
    slots = nb_ref.shape[0]

    sec, ctx, head = (lax.axis_index(a) for a in ("sec", "ctx", "head"))
    upper = ctx >= half
    mine = lax.rem(ctx, half)
    base = ctx - mine
    partner = lax.rem(ctx + half, n_ctx)
    within = sec * n_head + head

    def member(d):
        other = lax.rem(within + d, group)
        return other, {"sec": other // n_head, "head": lax.rem(other, n_head)}

    def flipped(d):
        place, bit = mine, 1
        while bit <= d:
            if d & bit:
                place = place + bit - 2 * bit * lax.rem(place // bit, 2)
            bit *= 2
        return place

    def last_bit(d, h, t):
        bits = [1 << i for i in range(d.bit_length()) if d >> i & 1]
        return bits[-1] if t == 1 and h % 2 == 1 else bits[0]

    def peer(d):
        return base + flipped(d)

    def cols(h):
        return slice(h * HD, (h + 1) * HD)

    barrier = pltpu.get_barrier_semaphore()
    for d in range(1, half):
        pl.semaphore_signal(barrier, inc=1, device_id={"ctx": peer(d)}, device_id_type=MESH)
    pl.semaphore_signal(barrier, inc=1, device_id={"ctx": partner}, device_id_type=MESH)
    for d in range(1, group):
        pl.semaphore_signal(barrier, inc=1, device_id=member(d)[1], device_id_type=MESH)

    own_start = pl.multiple_of(within * (2 * width), 2 * width)
    loads = [
        pltpu.make_async_copy(source, target, load.at[i])
        for i, (source, target) in enumerate(
            (
                (qs_hbm, qs_ref),
                (k_ref, k_all.at[mine]),
                (v_ref, v_all.at[mine]),
                (qc_hbm, qc_ref),
                (
                    nb_ref.at[:, :, pl.ds(own_start, 2 * width)],
                    nb_all.at[pl.ds(within * slots, slots)],
                ),
            )
        )
    ]
    for copy in loads:
        copy.start()
    pl.semaphore_wait(barrier, half - 1 + 1 + group - 1)

    def q_copy(h):
        return pltpu.make_async_remote_copy(
            src_ref=qs_hbm.at[:, cols(h)],
            dst_ref=q_in.at[:, cols(h)],
            send_sem=q_send.at[h],
            recv_sem=q_recv.at[h],
            device_id={"ctx": partner},
            device_id_type=MESH,
        )

    def kv_copy(d, h, t):
        own, gathered = ((k_ref, k_all), (v_ref, v_all))[t]
        bit = last_bit(d, h, t)
        origin = flipped(d - bit)
        source = own if d == bit else gathered.at[origin]
        return pltpu.make_async_remote_copy(
            src_ref=source.at[:, cols(h)],
            dst_ref=gathered.at[origin, :, cols(h)],
            send_sem=kv_send.at[d - 1, h, t],
            recv_sem=kv_recv.at[d - 1, h, t],
            device_id={"ctx": peer(bit)},
            device_id_type=MESH,
        )

    def o_copy(h, t):
        source, target = ((o_part.at[:, cols(h)], o_in.at[:, cols(h)]), (l_part.at[h], l_in.at[h]))[t]
        return pltpu.make_async_remote_copy(
            src_ref=source,
            dst_ref=target,
            send_sem=o_send.at[h, t],
            recv_sem=o_recv.at[h, t],
            device_id={"ctx": partner},
            device_id_type=MESH,
        )

    def nb_copy(d):
        other, place = member(d)
        start = pl.multiple_of(other * (2 * width), 2 * width)
        return pltpu.make_async_remote_copy(
            src_ref=nb_ref.at[:, :, pl.ds(start, 2 * width)],
            dst_ref=nb_all.at[pl.ds(within * slots, slots)],
            send_sem=nb_send.at[d - 1],
            recv_sem=nb_recv.at[d - 1],
            device_id=place,
            device_id_type=MESH,
        )

    offsets = sorted(range(1, half), key=lambda d: (d.bit_count(), d))
    arrived = set()

    def wait_kv(d, h, t):
        if (d, h, t) not in arrived:
            arrived.add((d, h, t))
            kv_copy(d, h, t).wait_recv()

    def send_own(h):
        pl.when(upper)(lambda: q_copy(h).start())
        for d in offsets:
            if d.bit_count() == 1:
                for t in range(2):
                    kv_copy(d, h, t).start()

    def send_on(h):
        for d in offsets:
            if d.bit_count() > 1:
                for t in range(2):
                    wait_kv(d - last_bit(d, h, t), h, t)
                    kv_copy(d, h, t).start()

    for h in range(min(AHEAD, heads)):
        send_own(h)
        if h == 0:
            for d in range(1, group):
                nb_copy(d).start()
    for copy in loads[:3]:
        copy.wait()

    def gathered_head(h):
        keys = k_all[:, :, cols(h)].reshape(half * rows, HD)
        values = v_all[:, :, cols(h)].reshape(half * rows, HD)
        return keys, values

    def attend_own(h):
        keys, values = gathered_head(h)
        place = lax.broadcasted_iota(jnp.int32, (rows, half * rows), 1)
        position = lax.broadcasted_iota(jnp.int32, (rows, half * rows), 0) + mine * rows
        return attend(qs_ref[:, cols(h)], keys, values, place <= position)

    def cross():
        for copy in loads[3:]:
            copy.wait()
        for d in range(1, group):
            nb_copy(d).wait_recv()
        for c in range(rows // STRETCH):
            picks = [map_ref[r, c] for r in range(map_ref.shape[0])]
            part = slice(c * STRETCH, (c + 1) * STRETCH)
            keep = jnp.logical_or(ctx > 0, c > 0)
            for h in range(heads):
                keys = jnp.concatenate([nb_all[v, :, cols(h)] for v in picks], axis=0)
                values = jnp.concatenate([nb_all[v, :, cols(heads + h)] for v in picks], axis=0)
                summed, _, total = attend(qc_ref[part, cols(h)], keys, values)
                co_ref[part, cols(h)] = jnp.where(keep, summed / total, 0.0).astype(co_ref.dtype)

    def serve(h):
        q_copy(h).wait_recv()
        keys, values = gathered_head(h)
        summed, top, total = attend(q_in[:, cols(h)], keys, values)
        o_part[:, cols(h)] = (summed / total).astype(o_part.dtype)
        level = jnp.broadcast_to(top + jnp.log2(total), (rows, HD))
        l_part[h] = jnp.transpose(level)[:8]
        for t in range(2):
            o_copy(h, t).start()

    def keep(h):
        summed, top, total = attend_own(h)
        own_sum[h] = summed
        own_top[h] = jnp.broadcast_to(top, (rows, HD))
        own_total[h] = jnp.broadcast_to(total, (rows, HD))

    def finish(h):
        summed, _, total = attend_own(h)
        so_ref[:, cols(h)] = (summed / total).astype(so_ref.dtype)

    def merge(h):
        for t in range(2):
            o_copy(h, t).wait_recv()
        level = jnp.transpose(jnp.broadcast_to(l_in[h, 0:1], (HD, rows)))
        top = own_top[h]
        peak = jnp.maximum(top, level)
        own, far = jnp.exp2(top - peak), jnp.exp2(level - peak)
        summed = own_sum[h] * own + o_in[:, cols(h)].astype(jnp.float32) * far
        so_ref[:, cols(h)] = (summed / (own_total[h] * own + far)).astype(so_ref.dtype)

    lower = jnp.logical_not(upper)
    for h in range(heads):
        if h == heads - 1:
            cross()
            pltpu.make_async_copy(co_ref, co_hbm, store.at[1]).start()
        for later in (range(min(2, heads)) if h == 0 else range(h + 1, min(h + 2, heads))):
            send_on(later)
            if later + AHEAD < heads:
                send_own(later + AHEAD)
        for d in offsets:
            for t in range(2):
                wait_kv(d, h, t)
        pl.when(lower)(lambda: serve(h))
        pl.when(lower)(lambda: finish(h))
        pl.when(upper)(lambda: keep(h))
    @pl.when(upper)
    def _():
        for h in range(heads):
            merge(h)
            q_copy(h).wait_send()

    @pl.when(lower)
    def _():
        for h in range(heads):
            for t in range(2):
                o_copy(h, t).wait_send()

    pltpu.make_async_copy(so_ref, so_hbm, store.at[0]).start()
    for h in range(heads):
        for d in range(1, half):
            for t in range(2):
                kv_copy(d, h, t).wait_send()
    for d in range(1, group):
        nb_copy(d).wait_send()
    pltpu.make_async_copy(so_ref, so_hbm, store.at[0]).wait()
    pltpu.make_async_copy(co_ref, co_hbm, store.at[1]).wait()


def on_device(sizes, query_self, key_self, value_self, query_cross, neighbour_kv, neighbour_map):
    rows, width = query_self.shape
    heads = width // HD
    half = sizes[1] // 2
    group = sizes[0] * sizes[2]
    slots, block_len, _ = neighbour_kv.shape
    bf16, f32 = jnp.bfloat16, jnp.float32
    anywhere = pl.BlockSpec(memory_space=pl.ANY)
    out = jax.ShapeDtypeStruct((rows, width), bf16)
    pairs = rows * rows * heads * (2 * half)
    return pl.pallas_call(
        functools.partial(kernel, sizes),
        out_shape=(out, out),
        in_specs=[pl.BlockSpec(memory_space=pltpu.SMEM)]
        + [anywhere] * 5,
        out_specs=(anywhere, anywhere),
        scratch_shapes=[
            pltpu.VMEM((rows, width), bf16),
            pltpu.VMEM((rows, width), bf16),
            pltpu.VMEM((rows, width), bf16),
            pltpu.VMEM((rows, width), bf16),
            pltpu.VMEM((half, rows, width), bf16),
            pltpu.VMEM((half, rows, width), bf16),
            pltpu.VMEM((rows, width), bf16),
            pltpu.VMEM((rows, width), bf16),
            pltpu.VMEM((heads, 8, rows), f32),
            pltpu.VMEM((rows, width), bf16),
            pltpu.VMEM((heads, 8, rows), f32),
            pltpu.VMEM((heads, rows, HD), f32),
            pltpu.VMEM((heads, rows, HD), f32),
            pltpu.VMEM((heads, rows, HD), f32),
            pltpu.VMEM((group * slots, block_len, 2 * width), bf16),
            pltpu.SemaphoreType.DMA((half - 1, heads, 2)),
            pltpu.SemaphoreType.DMA((half - 1, heads, 2)),
            pltpu.SemaphoreType.DMA((heads,)),
            pltpu.SemaphoreType.DMA((heads,)),
            pltpu.SemaphoreType.DMA((heads, 2)),
            pltpu.SemaphoreType.DMA((heads, 2)),
            pltpu.SemaphoreType.DMA((group - 1,)),
            pltpu.SemaphoreType.DMA((group - 1,)),
            pltpu.SemaphoreType.DMA((5,)),
            pltpu.SemaphoreType.DMA((2,)),
        ],
        compiler_params=pltpu.CompilerParams(
            collective_id=0, has_side_effects=True, vmem_limit_bytes=56 * 1024 * 1024
        ),
        cost_estimate=pl.CostEstimate(
            flops=4 * pairs * HD, bytes_accessed=2 * 1024 * 1024, transcendentals=pairs
        ),
    )(jnp.transpose(neighbour_map), query_self, key_self, value_self, query_cross, neighbour_kv)


def solution(mesh):
    sizes = tuple(mesh.shape[a] for a in ("sec", "ctx", "head"))
    split = P("ctx", ("sec", "head"))
    return jax.shard_map(
        functools.partial(on_device, sizes),
        mesh=mesh,
        in_specs=(split, split, split, split, P(("sec", "ctx", "head"), None, None), P("ctx", None)),
        out_specs=(split, split),
        check_vma=False,
    )
```
